32 devices in a mesh: parts: 2 (over x), blk: 2 (over core), rows: 8 (over z, y).
Axes of the slice: x: 2, y: 2, z: 4, core: 2. Of those that a mesh axis runs over, the one named last changes fastest.
Arguments:
- wave: bfloat16 [2, 1024, 128, 128], P('blk', ('parts', 'rows')), parts along dimension 1, may hold values from -6 to 6
- left_env: bfloat16 [256, 10, 128, 128], P(('parts', 'rows'), 'blk'), parts along dimension 0, may hold values from -0.5 to 0.5
- right_env: bfloat16 [256, 10, 128, 128], P(('parts', 'rows'), 'blk'), parts along dimension 0, may hold values from -0.25 to 0.25
- right_slot: int32 [1024], P('parts'), parts along dimension 0, may hold values from 0 to 511, as said below
- term_mask: int32 [256, 10], P(('parts', 'rows')), parts along dimension 0, may hold values from 0 to 1, as said below
Outputs:
- applied: bfloat16 [2, 1024, 128, 128], P('blk', ('parts', 'rows')), parts along dimension 1
The draws below stay inside these ranges and needn't reach their ends.
There are 2 independent parts, one for each index of `parts`. The reference program is written for one: setup_inputs(seed, part) draws one part's arguments, and reference() takes and returns one part's arrays. A program takes and returns all parts, laid end to end along the dimension named above; each array names one. Nothing has to cross between parts.
Inputs may be any that keep to these rules, and one draw needn't show every extreme that they name: right_slot is a permutation of the blocks; block b lies on index b // 64 of rows and goes to index right_slot[b] // 64; every index of rows receives 4 * 16 blocks, sends at most 8 of them to any one index, and sends exactly 8 to some. `term_mask`: every row holds exactly 5 ones.
All inputs are finite; a program needn't handle non-finite values.
Results may differ from the reference program's by a relative error of at most 0.0049.
Values may be sent and summed in bfloat16 or wider, within the bound.
No kernel may reach another device: no remote copies, remote signals or barrier semaphores. Data moves between devices by JAX's collectives and lax.ppermute only.
A program may use at most 192 MiB of HBM per device.

```python
import jax
import jax.numpy as jnp
from jax import lax

Q = 128
W = 10
WACT = 5
FAN = 4
SEC_DEV = 16
NV = 2
NSEC = 128
NB = 512


def draw_right_slot(key, part):
    key = jax.random.fold_in(key, 11)
    per_device = FAN * SEC_DEV
    devices = NB // per_device
    key_send, key_recv, key_place = jax.random.split(key, 3)
    senders = jax.random.permutation(key_send, devices)
    receivers = jax.random.permutation(key_recv, devices)
    scores = jax.random.randint(key_place, (devices, per_device), 0, 1 << 20) * per_device + jnp.arange(per_device)[None, :]
    places = jnp.argsort(scores, axis=1)
    sender = jnp.arange(devices)[:, None]
    member = jnp.arange(per_device)[None, :]
    target = receivers[(senders[sender] + member) % devices]
    slots_out = target * per_device + places[target, member]
    return slots_out.reshape(-1).astype(jnp.int32)


def draw_term_mask(key, part):
    key = jax.random.fold_in(key, 12)
    scores = jax.random.randint(key, (NSEC, W), 0, 1 << 20) * W + jnp.arange(W)[None, :]
    ranking = jnp.argsort(jnp.argsort(scores, axis=1), axis=1)
    return (ranking < WACT).astype(jnp.int32)


def levels(key, dims, cuts, smallest, high):
    loudness, own = 1.0, jax.random.fold_in(key, 6)
    for axis_at, blocks in cuts:
        draws = jnp.exp(jax.random.uniform(jax.random.fold_in(own, axis_at), (blocks,), jnp.float32, smallest / len(cuts), high / len(cuts)))
        loudness = loudness * jnp.repeat(draws, dims[axis_at] // blocks).reshape([-1 if axis == axis_at else 1 for axis in range(len(dims))])
    return loudness


def centred(stream_key, extent, deviation, limit, cuts=(), held_as=jnp.bfloat16):
    array = deviation * jax.random.normal(stream_key, extent, jnp.float32)
    if cuts:
        array = array * levels(stream_key, extent, cuts, -0.22, 0.18)
    return jnp.clip(array, -limit, limit).astype(held_as)


def setup_inputs(seed: int = 0, part: int = 0) -> dict:
    key_of = jax.random.split(jax.random.key(seed), 6)
    own_keys = jax.random.split(jax.random.fold_in(key_of[5], part), 6)
    return {
        "wave": centred(own_keys[0], (NV, NB, Q, Q), 1.0, 6.0, ((0, 2), (1, 8))),
        "left_env": centred(own_keys[1], (NSEC, W, Q, Q), Q ** -0.5, 0.5, ((0, 8), (1, 2))),
        "right_env": centred(own_keys[2], (NSEC, W, Q, Q), (Q * WACT) ** -0.5, 0.25, ((0, 8), (1, 2))),
        "right_slot": draw_right_slot(jax.random.fold_in(jax.random.fold_in(key_of[5], part), 71), part),
        "term_mask": draw_term_mask(jax.random.fold_in(jax.random.fold_in(key_of[5], part), 71), part),
    }


def reference(wave, left_env, right_env, right_slot, term_mask):
    sectors = left_env.shape[0]
    fan_out = wave.shape[1] // sectors
    right_sector = (right_slot.reshape(sectors, fan_out) // fan_out).astype(jnp.int32)

    def one_sector(sector_index):
        wave_part = lax.dynamic_slice_in_dim(wave, sector_index * fan_out, fan_out, axis=1).astype(jnp.float32)
        left_part = left_env[sector_index].astype(jnp.float32)
        product = jnp.einsum("kab,vtbc->vtkac", left_part, wave_part, precision=lax.Precision.HIGHEST)
        product = lax.optimization_barrier(product.astype(jnp.bfloat16)).astype(jnp.float32)
        right_part = right_env[right_sector[sector_index]].astype(jnp.float32)
        term_row = term_mask[sector_index].astype(jnp.float32)
        applied = jnp.einsum("vtkac,tkdc,k->vtad", product, right_part, term_row, precision=lax.Precision.HIGHEST)
        return applied.astype(jnp.bfloat16)

    per_sector = lax.map(one_sector, jnp.arange(sectors, dtype=jnp.int32))
    vectors = wave.shape[0]
    per_sector = jnp.transpose(per_sector, (1, 0, 2, 3, 4))
    return per_sector.reshape(vectors, wave.shape[1], wave.shape[2], wave.shape[3])
```

```python
import functools

import jax
import jax.numpy as jnp
from jax import lax
from jax.experimental import pallas as pl
from jax.experimental.pallas import tpu as pltpu
from jax.sharding import PartitionSpec as P

WACT = 5
VMEM = 48 * 1024 * 1024


def smem():
    return pl.BlockSpec(memory_space=pltpu.SMEM)


def hbm():
    return pl.BlockSpec(memory_space=pl.ANY)


class Plan:
    def __init__(self, wave, left_env, devices, cores):
        self.blocks, self.width = wave.shape[1], wave.shape[3]
        self.sectors, self.half = left_env.shape[0], left_env.shape[1]
        self.fan = self.blocks // self.sectors
        self.devices = devices
        self.cap = self.blocks // devices
        self.split = cores == 2 and self.cap % 2 == 0
        self.capc = self.cap // 2 if self.split else self.cap
        self.vectors = 2 if self.split else 1
        self.by_pairs = devices == 8
        if self.by_pairs:
            self.groups = [(4,), (5,), (6,), (7,), (2,), (3,), (1,), (0,)]
        else:
            self.groups = [tuple(range(devices))]

    def partner(self, p):
        return jnp.bitwise_xor(lax.axis_index("rows"), p) if self.by_pairs else jnp.int32(p)

    def rank0(self, core):
        return core * self.capc if self.split else 0


def lists(plan, right_slot):
    devices, blocks, cap, fan, sectors = plan.devices, plan.blocks, plan.cap, plan.fan, plan.sectors
    me = lax.axis_index("rows")
    slots = right_slot.reshape(devices, blocks)
    target = slots // blocks
    index = jnp.arange(blocks, dtype=jnp.int32)
    earlier = (target[:, None, :] == target[:, :, None]) & (index[None, None, :] < index[None, :, None])
    rank = jnp.sum(earlier.astype(jnp.int32), axis=2)
    ranks = jnp.arange(cap, dtype=jnp.int32)
    device = jnp.arange(devices, dtype=jnp.int32)
    value = (device[:, None] * sectors + index[None, :] // fan) * sectors + (slots % blocks) // fan
    hit = (target[:, None, :] == me) & (rank[:, None, :] == ranks[None, :, None])
    code = jnp.sum(jnp.where(hit, value[:, None, :], 0), axis=2)
    my_target = lax.dynamic_slice_in_dim(target, me, 1, axis=0)
    my_rank = lax.dynamic_slice_in_dim(rank, me, 1, axis=0)
    mine = (my_target[:, None, :] == device[:, None, None]) & (my_rank[:, None, :] == ranks[None, :, None])
    order = jnp.sum(jnp.where(mine, index[None, None, :], 0), axis=2)
    return order.astype(jnp.int32).reshape(-1), code.astype(jnp.int32).reshape(-1)


def active(term_mask):
    comps = term_mask.shape[1]
    k = jnp.arange(comps, dtype=jnp.int32)
    on = term_mask == 1
    before = jnp.sum((on[:, None, :] & (k[None, None, :] < k[None, :, None])).astype(jnp.int32), axis=2)
    j = jnp.arange(WACT, dtype=jnp.int32)
    chosen = on[:, None, :] & (before[:, None, :] == j[None, :, None])
    return jnp.sum(jnp.where(chosen, k[None, None, :], 0), axis=2).astype(jnp.int32)


def send_kernel(plan, groups, code_ref, comps_ref, own_ref, other_ref, *rest):
    outs, sem = rest[: len(groups)], rest[len(groups)]
    core = lax.axis_index("blk")
    for n, group in enumerate(groups):
        out = outs[n]

        @pl.loop(0, len(group) * plan.capc)
        def _(s):
            p = group[0] if len(group) == 1 else s // plan.capc
            q = s if len(group) == 1 else lax.rem(s, plan.capc)
            code = code_ref[plan.partner(p) * plan.cap + plan.rank0(core) + q]
            sector = lax.rem(code, plan.sectors)
            row = lax.div(code, plan.sectors)
            for j in range(WACT):
                k = comps_ref[row * WACT + j]
                side = lax.div(k, plan.half)
                at = lax.rem(k, plan.half)
                dst = out.at[s, j]

                @pl.when(side == core)
                def _():
                    pltpu.make_async_copy(own_ref.at[sector, at], dst, sem.at[n]).start()

                @pl.when(side != core)
                def _():
                    pltpu.make_async_copy(other_ref.at[sector, at], dst, sem.at[n]).start()

    for n in range(len(groups)):
        pltpu.make_async_copy(outs[n], outs[n], sem.at[n]).wait()


def send(plan, groups, code, comps, own, other):
    w = plan.width
    return pl.pallas_call(
        functools.partial(send_kernel, plan, groups),
        out_shape=[jax.ShapeDtypeStruct((len(g) * plan.capc, WACT, w, w), own.dtype) for g in groups],
        in_specs=[smem(), smem(), hbm(), hbm()],
        out_specs=[hbm() for _ in groups],
        scratch_shapes=[pltpu.SemaphoreType.DMA((len(groups),))],
        cost_estimate=pl.CostEstimate(flops=0, bytes_accessed=2 * len(groups) * len(groups[0]) * plan.capc * WACT * w * w * 2, transcendentals=0),
    )(code, comps, own, other)


def product_kernel(plan, order_ref, comps_ref, own_l, other_l, *rest):
    waves, (out_ref, left, psi, sem) = rest[: plan.vectors], rest[plan.vectors :]
    core = lax.axis_index("blk")
    s = pl.program_id(0)
    w = plan.width

    @pl.when(s == 0)
    def _():
        copies = [
            pltpu.make_async_copy(own_l, left.at[:, pl.ds(core * plan.half, plan.half)], sem.at[0]),
            pltpu.make_async_copy(other_l, left.at[:, pl.ds((1 - core) * plan.half, plan.half)], sem.at[1]),
        ]
        for v in range(plan.vectors):
            copies.append(pltpu.make_async_copy(waves[v], psi.at[v], sem.at[2 + v]))
        for c in copies:
            c.start()
        for c in copies:
            c.wait()

    p, q = lax.div(s, plan.capc), lax.rem(s, plan.capc)
    b = order_ref[plan.partner(p) * plan.cap + plan.rank0(core) + q]
    sector = lax.div(b, plan.fan)
    lhs = jnp.concatenate([left[sector, comps_ref[sector * WACT + j]] for j in range(WACT)], axis=0)
    rhs = jnp.concatenate([psi[v, b] for v in range(plan.vectors)], axis=1)
    terms = jnp.dot(lhs, rhs, preferred_element_type=jnp.float32).astype(jnp.bfloat16)
    for j in range(WACT):
        for v in range(plan.vectors):
            out_ref[0, pl.ds(v * w, w), pl.ds(j * w, w)] = terms[j * w : (j + 1) * w, v * w : (v + 1) * w]


def products(plan, order, comps, own_l, other_l, waves):
    w, slots = plan.width, plan.devices * plan.capc
    return pl.pallas_call(
        functools.partial(product_kernel, plan),
        grid=(slots,),
        out_shape=jax.ShapeDtypeStruct((slots, plan.vectors * w, WACT * w), jnp.bfloat16),
        in_specs=[smem(), smem(), hbm(), hbm()] + [hbm() for _ in waves],
        out_specs=pl.BlockSpec((1, plan.vectors * w, WACT * w), lambda s: (s, 0, 0)),
        scratch_shapes=[
            pltpu.VMEM((plan.sectors, 2 * plan.half, w, w), jnp.bfloat16),
            pltpu.VMEM((plan.vectors, plan.blocks, w, w), jnp.bfloat16),
            pltpu.SemaphoreType.DMA((2 + plan.vectors,)),
        ],
        compiler_params=pltpu.CompilerParams(vmem_limit_bytes=VMEM),
        cost_estimate=pl.CostEstimate(
            flops=2 * slots * plan.vectors * WACT * w**3,
            bytes_accessed=slots * plan.vectors * WACT * w * w * 2 + 9_000_000,
            transcendentals=0,
        ),
    )(order, comps, own_l, other_l, *waves)


def contract_kernel(plan, terms_ref, right_ref, *outs):
    w = plan.width
    right = jnp.concatenate([right_ref[0, j] for j in range(WACT)], axis=1)
    done = lax.dot_general(
        terms_ref[0], right, (((1,), (1,)), ((), ())), preferred_element_type=jnp.float32
    ).astype(jnp.bfloat16)
    for v in range(plan.vectors):
        outs[v][0] = done[v * w : (v + 1) * w]


def contract(plan, group, terms, right):
    w, count = plan.width, len(group) * plan.capc
    first = group[0] * plan.capc
    return pl.pallas_call(
        functools.partial(contract_kernel, plan),
        grid=(count,),
        out_shape=[jax.ShapeDtypeStruct((count, w, w), jnp.bfloat16) for _ in range(plan.vectors)],
        in_specs=[
            pl.BlockSpec((1, plan.vectors * w, WACT * w), lambda s: (first + s, 0, 0)),
            pl.BlockSpec((1, WACT, w, w), lambda s: (s, 0, 0, 0)),
        ],
        out_specs=[pl.BlockSpec((1, w, w), lambda s: (s, 0, 0)) for _ in range(plan.vectors)],
        compiler_params=pltpu.CompilerParams(vmem_limit_bytes=VMEM),
        cost_estimate=pl.CostEstimate(
            flops=2 * count * plan.vectors * WACT * w**3,
            bytes_accessed=count * (plan.vectors + 1) * (WACT + 1) * w * w * 2,
            transcendentals=0,
        ),
    )(terms, right)


def place_kernel(plan, order_ref, *rest):
    n = len(plan.groups)
    parts, out_ref, sem = rest[: n * plan.vectors], rest[n * plan.vectors], rest[n * plan.vectors + 1]
    core = lax.axis_index("blk")
    for v in range(plan.vectors):
        whose = core if v == 0 else 1 - core
        for g, group in enumerate(plan.groups):
            part = parts[v * n + g]

            @pl.loop(0, len(group) * plan.capc)
            def _(s):
                p = group[0] if len(group) == 1 else s // plan.capc
                q = s if len(group) == 1 else lax.rem(s, plan.capc)
                b = order_ref[plan.partner(p) * plan.cap + plan.rank0(whose) + q]
                pltpu.make_async_copy(part.at[s], out_ref.at[b], sem).start()

    pltpu.make_async_copy(out_ref, out_ref, sem).wait()


def place(plan, order, parts):
    w = plan.width
    return pl.pallas_call(
        functools.partial(place_kernel, plan),
        out_shape=jax.ShapeDtypeStruct((plan.blocks, w, w), jnp.bfloat16),
        in_specs=[smem()] + [hbm() for _ in parts],
        out_specs=hbm(),
        scratch_shapes=[pltpu.SemaphoreType.DMA],
        cost_estimate=pl.CostEstimate(flops=0, bytes_accessed=2 * plan.blocks * w * w * 2, transcendentals=0),
    )(order, *parts)


def body(wave, left_env, right_env, right_slot, term_mask):
    devices = lax.axis_size("rows")
    plan = Plan(wave, left_env, devices, lax.axis_size("blk"))
    swap = functools.partial(lax.ppermute, axis_name="blk", perm=[(0, 1), (1, 0)])

    other_r = swap(right_env)
    comps = active(term_mask).reshape(-1)
    asked = lax.all_to_all(
        jnp.broadcast_to(comps[None], (devices, comps.shape[0])), "rows", split_axis=0, concat_axis=0, tiled=True
    ).reshape(-1)
    order, code = lists(plan, right_slot)

    groups = plan.groups
    sent = []
    for some in (groups[:2], groups[2:]):
        if some:
            sent += send(plan, some, code, asked, right_env, other_r)
    if plan.by_pairs:
        right = [
            x if g == (0,) else lax.ppermute(x, "rows", [(i, i ^ g[0]) for i in range(devices)])
            for g, x in zip(groups, sent)
        ]
    else:
        right = [lax.all_to_all(sent[0], "rows", split_axis=0, concat_axis=0, tiled=True)]

    other_l = swap(left_env)
    waves = [wave[0]] + ([swap(wave[0])] if plan.split else [])
    terms = products(plan, order, comps, left_env, other_l, waves)
    done = [contract(plan, g, terms, r) for g, r in zip(groups, right)]
    parts = [d[0] for d in done]
    if plan.split:
        parts += [swap(d[1]) for d in done]
    return place(plan, order, parts)[None]


def solution(mesh):
    in_specs = (
        P("blk", ("parts", "rows"), None, None),
        P(("parts", "rows"), "blk", None, None),
        P(("parts", "rows"), "blk", None, None),
        P("parts"),
        P(("parts", "rows"), None),
    )
    out_specs = P("blk", ("parts", "rows"), None, None)
    return jax.shard_map(body, mesh=mesh, in_specs=in_specs, out_specs=out_specs, check_vma=False)
```

```python
import functools

import jax
import jax.numpy as jnp
from jax import lax
from jax.experimental import pallas as pl
from jax.experimental.pallas import tpu as pltpu
from jax.sharding import PartitionSpec as P

WACT = 5
VMEM = 48 * 1024 * 1024


def smem():
    return pl.BlockSpec(memory_space=pltpu.SMEM)


def vmem():
    return pl.BlockSpec(memory_space=pltpu.VMEM)


def hbm():
    return pl.BlockSpec(memory_space=pl.ANY)


class Plan:
    def __init__(self, wave, left_env, devices, cores):
        self.blocks, self.width = wave.shape[1], wave.shape[3]
        self.sectors, self.half = left_env.shape[0], left_env.shape[1]
        self.fan = self.blocks // self.sectors
        self.devices = devices
        self.cap = self.blocks // devices
        self.split = cores == 2 and self.cap % 2 == 0
        self.capc = self.cap // 2 if self.split else self.cap
        self.vectors = 2 if self.split else 1
        self.by_pairs = devices == 8
        if self.by_pairs:
            self.groups = [(4,), (5,), (6,), (7,), (2,), (3,), (1,), (0,)]
        else:
            self.groups = [tuple(range(devices))]

    def partner(self, p):
        return jnp.bitwise_xor(lax.axis_index("rows"), p) if self.by_pairs else jnp.int32(p)

    def rank0(self, core):
        return core * self.capc if self.split else 0


def lists(plan, right_slot):
    devices, blocks, cap, fan, sectors = plan.devices, plan.blocks, plan.cap, plan.fan, plan.sectors
    me = lax.axis_index("rows")
    slots = right_slot.reshape(devices, blocks)
    target = slots // blocks
    index = jnp.arange(blocks, dtype=jnp.int32)
    earlier = (target[:, None, :] == target[:, :, None]) & (index[None, None, :] < index[None, :, None])
    rank = jnp.sum(earlier.astype(jnp.int32), axis=2)
    ranks = jnp.arange(cap, dtype=jnp.int32)
    device = jnp.arange(devices, dtype=jnp.int32)
    value = (device[:, None] * sectors + index[None, :] // fan) * sectors + (slots % blocks) // fan
    hit = (target[:, None, :] == me) & (rank[:, None, :] == ranks[None, :, None])
    code = jnp.sum(jnp.where(hit, value[:, None, :], 0), axis=2)
    my_target = lax.dynamic_slice_in_dim(target, me, 1, axis=0)
    my_rank = lax.dynamic_slice_in_dim(rank, me, 1, axis=0)
    mine = (my_target[:, None, :] == device[:, None, None]) & (my_rank[:, None, :] == ranks[None, :, None])
    order = jnp.sum(jnp.where(mine, index[None, None, :], 0), axis=2)
    return order.astype(jnp.int32).reshape(-1), code.astype(jnp.int32).reshape(-1)


def active(term_mask):
    comps = term_mask.shape[1]
    k = jnp.arange(comps, dtype=jnp.int32)
    on = term_mask == 1
    before = jnp.sum((on[:, None, :] & (k[None, None, :] < k[None, :, None])).astype(jnp.int32), axis=2)
    j = jnp.arange(WACT, dtype=jnp.int32)
    chosen = on[:, None, :] & (before[:, None, :] == j[None, :, None])
    return jnp.sum(jnp.where(chosen, k[None, None, :], 0), axis=2).astype(jnp.int32)


def each(count, step):
    if count <= 8:
        for s in range(count):
            step(s)
    else:
        pl.loop(0, count)(step)


def slot(plan, group, s):
    if len(group) == 1:
        return group[0], s
    return lax.div(s, plan.capc), lax.rem(s, plan.capc)


def send_kernel(plan, groups, code_ref, *rest):
    n = len(groups)
    asked, (own_ref, other_ref), outs = rest[:n], rest[n : n + 2], rest[n + 2 :]
    core = lax.axis_index("blk")
    for group, comps_ref, out in zip(groups, asked, outs):

        def step(s):
            p, q = slot(plan, group, s)
            code = code_ref[plan.partner(p) * plan.cap + plan.rank0(core) + q]
            sector = lax.rem(code, plan.sectors)
            row = lax.div(code, plan.sectors)
            if len(group) == 1:
                row = lax.rem(row, plan.sectors)
            for j in range(WACT):
                k = comps_ref[row * WACT + j]
                mine = lax.div(k, plan.half) == core
                at = lax.rem(k, plan.half)
                out[s, j] = jnp.where(mine, own_ref[sector, at], other_ref[sector, at])

        each(len(group) * plan.capc, step)


def send(plan, groups, code, asked, own, other):
    w = plan.width
    return pl.pallas_call(
        functools.partial(send_kernel, plan, groups),
        out_shape=[jax.ShapeDtypeStruct((len(g) * plan.capc, WACT, w, w), own.dtype) for g in groups],
        in_specs=[smem()] + [smem() for _ in groups] + [vmem(), vmem()],
        out_specs=[vmem() for _ in groups],
        compiler_params=pltpu.CompilerParams(vmem_limit_bytes=VMEM),
        cost_estimate=pl.CostEstimate(flops=0, bytes_accessed=8_000_000, transcendentals=0),
    )(code, *asked, own, other)


def product_kernel(plan, order_ref, comps_ref, own_l, other_l, *rest):
    waves, (out_ref, left, psi, sem) = rest[: plan.vectors], rest[plan.vectors :]
    core = lax.axis_index("blk")
    s = pl.program_id(0)
    w = plan.width

    @pl.when(s == 0)
    def _():
        copies = [
            pltpu.make_async_copy(own_l, left.at[:, pl.ds(core * plan.half, plan.half)], sem.at[0]),
            pltpu.make_async_copy(other_l, left.at[:, pl.ds((1 - core) * plan.half, plan.half)], sem.at[1]),
        ]
        for v in range(plan.vectors):
            copies.append(pltpu.make_async_copy(waves[v], psi.at[v], sem.at[2 + v]))
        for c in copies:
            c.start()
        for c in copies:
            c.wait()

    p, q = lax.div(s, plan.capc), lax.rem(s, plan.capc)
    b = order_ref[plan.partner(p) * plan.cap + plan.rank0(core) + q]
    sector = lax.div(b, plan.fan)
    lhs = jnp.concatenate([left[sector, comps_ref[sector * WACT + j]] for j in range(WACT)], axis=0)
    rhs = jnp.concatenate([psi[v, b] for v in range(plan.vectors)], axis=1)
    terms = jnp.dot(lhs, rhs, preferred_element_type=jnp.float32).astype(jnp.bfloat16)
    for j in range(WACT):
        for v in range(plan.vectors):
            out_ref[0, pl.ds(v * w, w), pl.ds(j * w, w)] = terms[j * w : (j + 1) * w, v * w : (v + 1) * w]


def products(plan, order, comps, own_l, other_l, waves):
    w, slots = plan.width, plan.devices * plan.capc
    return pl.pallas_call(
        functools.partial(product_kernel, plan),
        grid=(slots,),
        out_shape=jax.ShapeDtypeStruct((slots, plan.vectors * w, WACT * w), jnp.bfloat16),
        in_specs=[smem(), smem(), hbm(), hbm()] + [hbm() for _ in waves],
        out_specs=pl.BlockSpec((1, plan.vectors * w, WACT * w), lambda s: (s, 0, 0)),
        scratch_shapes=[
            pltpu.VMEM((plan.sectors, 2 * plan.half, w, w), jnp.bfloat16),
            pltpu.VMEM((plan.vectors, plan.blocks, w, w), jnp.bfloat16),
            pltpu.SemaphoreType.DMA((2 + plan.vectors,)),
        ],
        compiler_params=pltpu.CompilerParams(vmem_limit_bytes=VMEM),
        cost_estimate=pl.CostEstimate(
            flops=2 * slots * plan.vectors * WACT * w**3,
            bytes_accessed=slots * plan.vectors * WACT * w * w * 2 + 9_000_000,
            transcendentals=0,
        ),
    )(order, comps, own_l, other_l, *waves)


def contract_kernel(plan, terms_ref, right_ref, *outs):
    w = plan.width
    right = jnp.concatenate([right_ref[0, j] for j in range(WACT)], axis=1)
    done = lax.dot_general(
        terms_ref[0], right, (((1,), (1,)), ((), ())), preferred_element_type=jnp.float32
    ).astype(jnp.bfloat16)
    for v in range(plan.vectors):
        outs[v][0] = done[v * w : (v + 1) * w]


def contract(plan, group, terms, right):
    w, count = plan.width, len(group) * plan.capc
    first = group[0] * plan.capc
    return pl.pallas_call(
        functools.partial(contract_kernel, plan),
        grid=(count,),
        out_shape=[jax.ShapeDtypeStruct((count, w, w), jnp.bfloat16) for _ in range(plan.vectors)],
        in_specs=[
            pl.BlockSpec((1, plan.vectors * w, WACT * w), lambda s: (first + s, 0, 0)),
            pl.BlockSpec((1, WACT, w, w), lambda s: (s, 0, 0, 0)),
        ],
        out_specs=[pl.BlockSpec((1, w, w), lambda s: (s, 0, 0)) for _ in range(plan.vectors)],
        compiler_params=pltpu.CompilerParams(vmem_limit_bytes=VMEM),
        cost_estimate=pl.CostEstimate(
            flops=2 * count * plan.vectors * WACT * w**3,
            bytes_accessed=count * (plan.vectors + 1) * (WACT + 1) * w * w * 2,
            transcendentals=0,
        ),
    )(terms, right)


def place_kernel(plan, order_ref, *rest):
    n = len(plan.groups)
    parts, out_ref = rest[:-1], rest[-1]
    core = lax.axis_index("blk")
    for v in range(plan.vectors):
        whose = core if v == 0 else 1 - core
        for g, group in enumerate(plan.groups):
            part = parts[v * n + g]

            def step(s):
                p, q = slot(plan, group, s)
                b = order_ref[plan.partner(p) * plan.cap + plan.rank0(whose) + q]
                out_ref[b] = part[s]

            each(len(group) * plan.capc, step)


def place(plan, order, parts):
    w = plan.width
    return pl.pallas_call(
        functools.partial(place_kernel, plan),
        out_shape=jax.ShapeDtypeStruct((plan.blocks, w, w), jnp.bfloat16),
        in_specs=[smem()] + [vmem() for _ in parts],
        out_specs=vmem(),
        compiler_params=pltpu.CompilerParams(vmem_limit_bytes=VMEM),
        cost_estimate=pl.CostEstimate(flops=0, bytes_accessed=2 * plan.blocks * w * w * 2, transcendentals=0),
    )(order, *parts)


def body(wave, left_env, right_env, right_slot, term_mask):
    devices = lax.axis_size("rows")
    plan = Plan(wave, left_env, devices, lax.axis_size("blk"))
    swap = functools.partial(lax.ppermute, axis_name="blk", perm=[(0, 1), (1, 0)])

    other_r = swap(right_env)
    comps = active(term_mask).reshape(-1)
    order, code = lists(plan, right_slot)
    groups = plan.groups

    def meet(x, group):
        if group == (0,):
            return x
        return lax.ppermute(x, "rows", [(i, i ^ group[0]) for i in range(devices)])

    if plan.by_pairs:
        asked = [meet(comps, g) for g in groups]
        sent = send(plan, groups[:2], code, asked[:2], right_env, other_r)
        sent += send(plan, groups[2:], code, asked[2:], right_env, other_r)
        right = [meet(x, g) for g, x in zip(groups, sent)]
    else:
        everyone = functools.partial(lax.all_to_all, axis_name="rows", split_axis=0, concat_axis=0, tiled=True)
        asked = everyone(jnp.broadcast_to(comps[None], (devices, comps.shape[0]))).reshape(-1)
        sent = send(plan, groups, code, [asked], right_env, other_r)
        right = [everyone(sent[0])]

    other_l = swap(left_env)
    waves = [wave[0]] + ([swap(wave[0])] if plan.split else [])
    terms = products(plan, order, comps, left_env, other_l, waves)
    done = [contract(plan, g, terms, r) for g, r in zip(groups, right)]
    parts = [d[0] for d in done]
    if plan.split:
        parts += [swap(d[1]) for d in done]
    return place(plan, order, parts)[None]


def solution(mesh):
    in_specs = (
        P("blk", ("parts", "rows"), None, None),
        P(("parts", "rows"), "blk", None, None),
        P(("parts", "rows"), "blk", None, None),
        P("parts"),
        P(("parts", "rows"), None),
    )
    out_specs = P("blk", ("parts", "rows"), None, None)
    return jax.shard_map(body, mesh=mesh, in_specs=in_specs, out_specs=out_specs, check_vma=False)
```

```python
import functools

import jax
import jax.numpy as jnp
from jax import lax
from jax.experimental import pallas as pl
from jax.experimental.pallas import tpu as pltpu
from jax.sharding import PartitionSpec as P

WACT = 5
MIB = 1024 * 1024
COST = 1000


def smem():
    return pl.BlockSpec(memory_space=pltpu.SMEM)


def vmem():
    return pl.BlockSpec(memory_space=pltpu.VMEM)


def hbm():
    return pl.BlockSpec(memory_space=pltpu.HBM)


class Plan:
    def __init__(self, wave, left_env, devices, cores):
        self.blocks, self.width = wave.shape[1], wave.shape[3]
        self.sectors, self.half = left_env.shape[0], left_env.shape[1]
        self.fan = self.blocks // self.sectors
        self.devices = devices
        self.cap = self.blocks // devices
        self.split = cores == 2 and self.cap % 2 == 0
        self.capc = self.cap // 2 if self.split else self.cap
        self.vectors = 2 if self.split else 1
        self.by_pairs = devices == 8
        if self.by_pairs:
            self.groups = [(0,), (6,), (7,), (1,), (2,), (4,), (3,), (5,)]
        else:
            self.groups = [tuple(range(devices))]

    def partner(self, p):
        return jnp.bitwise_xor(lax.axis_index("rows"), p) if self.by_pairs else jnp.int32(p)

    def rank0(self, core):
        return core * self.capc if self.split else 0


def lists(plan, right_slot):
    devices, blocks, cap, fan, sectors = plan.devices, plan.blocks, plan.cap, plan.fan, plan.sectors
    me = lax.axis_index("rows")
    slots = right_slot.reshape(devices, blocks)
    target = slots // blocks
    index = jnp.arange(blocks, dtype=jnp.int32)
    earlier = (target[:, None, :] == target[:, :, None]) & (index[None, None, :] < index[None, :, None])
    rank = jnp.sum(earlier.astype(jnp.int32), axis=2)
    ranks = jnp.arange(cap, dtype=jnp.int32)
    device = jnp.arange(devices, dtype=jnp.int32)
    value = (device[:, None] * sectors + index[None, :] // fan) * sectors + (slots % blocks) // fan
    hit = (target[:, None, :] == me) & (rank[:, None, :] == ranks[None, :, None])
    code = jnp.sum(jnp.where(hit, value[:, None, :], 0), axis=2)
    my_target = lax.dynamic_slice_in_dim(target, me, 1, axis=0)
    my_rank = lax.dynamic_slice_in_dim(rank, me, 1, axis=0)
    mine = (my_target[:, None, :] == device[:, None, None]) & (my_rank[:, None, :] == ranks[None, :, None])
    order = jnp.sum(jnp.where(mine, index[None, None, :], 0), axis=2)
    return order.astype(jnp.int32).reshape(-1), code.astype(jnp.int32).reshape(-1)


def decode(mask_ref, row, comps, found_ref):
    at = jnp.int32(0)
    for k in range(comps):
        found_ref[at] = jnp.int32(k)
        at = at + mask_ref[row, k]
    return [found_ref[j] for j in range(WACT)]


def each(count, step):
    if count <= 8:
        for s in range(count):
            step(s)
    else:
        pl.loop(0, count)(step)


def slot(plan, group, s):
    if len(group) == 1:
        return group[0], s
    return lax.div(s, plan.capc), lax.rem(s, plan.capc)


def send_kernel(plan, groups, where, masks, code_ref, *rest):
    mask_refs, (own_ref, other_ref) = rest[:masks], rest[masks : masks + 2]
    outs, (found, sem) = rest[masks + 2 : -2], rest[-2:]
    core = lax.axis_index("blk")
    for n, (group, (held, first), out) in enumerate(zip(groups, where, outs)):
        mask_ref = mask_refs[held]

        def step(s):
            p, q = slot(plan, group, s)
            code = code_ref[plan.partner(p) * plan.cap + plan.rank0(core) + q]
            sector = lax.rem(code, plan.sectors)
            row = lax.div(code, plan.sectors)
            if len(group) == 1:
                row = first * plan.sectors + lax.rem(row, plan.sectors)
            for j, k in enumerate(decode(mask_ref, row, 2 * plan.half, found)):
                mine = lax.div(k, plan.half) == core
                at = lax.rem(k, plan.half)

                @pl.when(mine)
                def _():
                    pltpu.make_async_copy(own_ref.at[sector, at], out.at[s, j], sem.at[n]).start()

                @pl.when(jnp.logical_not(mine))
                def _():
                    pltpu.make_async_copy(other_ref.at[sector, at], out.at[s, j], sem.at[n]).start()

        each(len(group) * plan.capc, step)
    for n, out in enumerate(outs):
        pltpu.make_async_copy(out, out, sem.at[n]).wait()


def send(plan, groups, where, code, masks, own, other):
    w, left_comps = plan.width, 2 * plan.half
    return pl.pallas_call(
        functools.partial(send_kernel, plan, groups, where, len(masks)),
        out_shape=[jax.ShapeDtypeStruct((len(g) * plan.capc, WACT, w, w), own.dtype) for g in groups],
        in_specs=[smem()] + [smem() for _ in masks] + [hbm(), hbm()],
        out_specs=[vmem() for _ in groups],
        scratch_shapes=[pltpu.SMEM((left_comps + 1,), jnp.int32), pltpu.SemaphoreType.DMA((len(groups),))],
        compiler_params=pltpu.CompilerParams(vmem_limit_bytes=58 * MIB),
        cost_estimate=pl.CostEstimate(flops=0, bytes_accessed=8_000_000, transcendentals=0),
    )(code, *masks, own, other)


def product_kernel(plan, late, order_ref, mask_ref, own_l, other_l, *rest):
    waves, outs, (left, psi, sem, found) = rest[: plan.vectors], rest[plan.vectors : -4], rest[-4:]
    core = lax.axis_index("blk")
    s = pl.program_id(0)
    w = plan.width

    @pl.when(s == 0)
    def _():
        copies = [
            pltpu.make_async_copy(own_l, left.at[:, pl.ds(core * plan.half, plan.half)], sem.at[0]),
            pltpu.make_async_copy(other_l, left.at[:, pl.ds((1 - core) * plan.half, plan.half)], sem.at[1]),
        ]
        for v in range(plan.vectors):
            copies.append(pltpu.make_async_copy(waves[v], psi.at[v], sem.at[2 + v]))
        for c in copies:
            c.start()
        for c in copies:
            c.wait()

    p, q = lax.div(s, plan.capc), lax.rem(s, plan.capc)
    b = order_ref[plan.partner(p) * plan.cap + plan.rank0(core) + q]
    sector = lax.div(b, plan.fan)
    lhs = jnp.concatenate([left[sector, k] for k in decode(mask_ref, sector, 2 * plan.half, found)], axis=0)
    rhs = jnp.concatenate([psi[v, b] for v in range(plan.vectors)], axis=1)
    terms = jnp.dot(lhs, rhs, preferred_element_type=jnp.float32).astype(jnp.bfloat16)

    def store(out_ref, at):
        for j in range(WACT):
            for v in range(plan.vectors):
                out_ref[at, pl.ds(v * w, w), pl.ds(j * w, w)] = terms[j * w : (j + 1) * w, v * w : (v + 1) * w]

    store(outs[0], 0)
    if late is not None:
        pl.when(p == late)(lambda: store(outs[1], q))


def products(plan, late, order, term_mask, own_l, other_l, waves):
    w, slots = plan.width, plan.devices * plan.capc
    tall, wide = plan.vectors * w, WACT * w
    shapes = [jax.ShapeDtypeStruct((slots, tall, wide), jnp.bfloat16)]
    specs = [pl.BlockSpec((1, tall, wide), lambda s: (s, 0, 0))]
    if late is not None:
        shapes.append(jax.ShapeDtypeStruct((plan.capc, tall, wide), jnp.bfloat16))
        specs.append(pl.BlockSpec((plan.capc, tall, wide), lambda s: (0, 0, 0)))
    return pl.pallas_call(
        functools.partial(product_kernel, plan, late),
        grid=(slots,),
        out_shape=shapes,
        in_specs=[smem(), smem(), hbm(), hbm()] + [hbm() for _ in waves],
        out_specs=specs,
        scratch_shapes=[
            pltpu.VMEM((plan.sectors, 2 * plan.half, w, w), jnp.bfloat16),
            pltpu.VMEM((plan.vectors, plan.blocks, w, w), jnp.bfloat16),
            pltpu.SemaphoreType.DMA((2 + plan.vectors,)),
            pltpu.SMEM((2 * plan.half + 1,), jnp.int32),
        ],
        compiler_params=pltpu.CompilerParams(vmem_limit_bytes=20 * MIB),
        cost_estimate=pl.CostEstimate(flops=COST, bytes_accessed=COST, transcendentals=0),
    )(order, term_mask, own_l, other_l, *waves)


def contract_kernel(plan, terms_ref, right_ref, *outs):
    w = plan.width

    def step(s):
        right = jnp.concatenate([right_ref[s, j] for j in range(WACT)], axis=1)
        done = lax.dot_general(
            terms_ref[s], right, (((1,), (1,)), ((), ())), preferred_element_type=jnp.float32
        ).astype(jnp.bfloat16)
        for v in range(plan.vectors):
            outs[v][s] = done[v * w : (v + 1) * w]

    each(terms_ref.shape[0], step)


def contract(plan, group, terms, right):
    w, count = plan.width, len(group) * plan.capc
    block = min(count, 4)
    first = 0 if terms.shape[0] == count else group[0] * plan.capc // block
    return pl.pallas_call(
        functools.partial(contract_kernel, plan),
        grid=(count // block,),
        out_shape=[jax.ShapeDtypeStruct((count, w, w), jnp.bfloat16) for _ in range(plan.vectors)],
        in_specs=[
            pl.BlockSpec((block, plan.vectors * w, WACT * w), lambda s: (first + s, 0, 0)),
            pl.BlockSpec((block, WACT, w, w), lambda s: (s, 0, 0, 0)),
        ],
        out_specs=[pl.BlockSpec((block, w, w), lambda s: (s, 0, 0)) for _ in range(plan.vectors)],
        compiler_params=pltpu.CompilerParams(vmem_limit_bytes=8 * MIB),
        cost_estimate=pl.CostEstimate(flops=COST, bytes_accessed=COST, transcendentals=0),
    )(terms, right)


def place_kernel(plan, groups, order_ref, *rest):
    n = len(groups)
    parts, out_ref = rest[:-1], rest[-1]
    core = lax.axis_index("blk")
    for v in range(plan.vectors):
        whose = core if v == 0 else 1 - core
        for g, group in enumerate(groups):
            part = parts[v * n + g]

            def step(s):
                p, q = slot(plan, group, s)
                b = order_ref[plan.partner(p) * plan.cap + plan.rank0(whose) + q]
                out_ref[b] = part[s]

            each(len(group) * plan.capc, step)


def place(plan, groups, order, parts):
    w = plan.width
    return pl.pallas_call(
        functools.partial(place_kernel, plan, groups),
        out_shape=jax.ShapeDtypeStruct((plan.blocks, w, w), jnp.bfloat16),
        in_specs=[smem()] + [vmem() for _ in parts],
        out_specs=vmem(),
        compiler_params=pltpu.CompilerParams(vmem_limit_bytes=16 * MIB),
        cost_estimate=pl.CostEstimate(flops=COST, bytes_accessed=COST, transcendentals=0),
    )(order, *parts)


def place_last_kernel(plan, group, order_ref, *rest):
    parts, out_ref, sem = rest[: plan.vectors], rest[-2], rest[-1]
    core = lax.axis_index("blk")
    for wait in (False, True):
        for v in range(plan.vectors):
            whose = core if v == 0 else 1 - core
            for s in range(plan.capc):
                b = order_ref[plan.partner(group[0]) * plan.cap + plan.rank0(whose) + s]
                copy = pltpu.make_async_copy(parts[v].at[s], out_ref.at[b], sem.at[v * plan.capc + s])
                if wait:
                    copy.wait()
                else:
                    copy.start()


def place_last(plan, group, order, parts, result):
    return pl.pallas_call(
        functools.partial(place_last_kernel, plan, group),
        out_shape=jax.ShapeDtypeStruct(result.shape, result.dtype),
        in_specs=[smem()] + [vmem() for _ in parts] + [hbm()],
        out_specs=hbm(),
        scratch_shapes=[pltpu.SemaphoreType.DMA((plan.vectors * plan.capc,))],
        input_output_aliases={1 + plan.vectors: 0},
        compiler_params=pltpu.CompilerParams(vmem_limit_bytes=4 * MIB),
        cost_estimate=pl.CostEstimate(flops=0, bytes_accessed=1_000_000, transcendentals=0),
    )(order, *parts, result)


def body(wave, left_env, right_env, right_slot, term_mask):
    devices = lax.axis_size("rows")
    plan = Plan(wave, left_env, devices, lax.axis_size("blk"))
    swap = functools.partial(lax.ppermute, axis_name="blk", perm=[(0, 1), (1, 0)])

    other_r = swap(right_env)
    order, code = lists(plan, right_slot)
    groups = plan.groups

    def meet(x, group):
        if group == (0,):
            return x
        return lax.ppermute(x, "rows", [(i, i ^ group[0]) for i in range(devices)])

    everyone = functools.partial(lax.all_to_all, axis_name="rows", split_axis=0, concat_axis=0, tiled=True)
    rows, comps = term_mask.shape
    if plan.by_pairs:
        pair = jnp.concatenate([term_mask, meet(term_mask, (1,))])
        quad = jnp.concatenate([pair, meet(pair, (6,))])
        near = meet(quad, (2,))
        urgent = [(6,), (7,)]
        made = dict(zip(urgent, send(plan, urgent, [(0, 2), (0, 3)], code, [quad], right_env, other_r)))
        code, made[(6,)] = lax.optimization_barrier((code, made[(6,)]))
        others = [(1,), (2,), (4,), (3,), (5,), (0,)]
        where = [(0, 1), (1, 0), (1, 2), (1, 1), (1, 3), (0, 0)]
        made.update(zip(others, send(plan, others, where, code, [quad, near], right_env, other_r)))
        after = {(5,): (6,)}
        arrived = {}
        for g in groups:
            x = made[g]
            if g in after:
                x, arrived[after[g]] = lax.optimization_barrier((x, arrived[after[g]]))
            arrived[g] = meet(x, g)
        right = [arrived[g] for g in groups]
    else:
        wide = jnp.broadcast_to(term_mask[None], (devices, rows, comps)).reshape(-1, comps)
        sent = send(plan, groups, [(0, 0)], code, [everyone(wide)], right_env, other_r)
        right = [everyone(sent[0])]

    other_l = swap(left_env)
    waves = [wave[0]] + ([swap(wave[0])] if plan.split else [])
    last = groups[-1]
    terms = products(plan, last[0] if plan.by_pairs else None, order, term_mask, left_env, other_l, waves)

    def finish(n):
        mine = terms[1] if plan.by_pairs and n == len(groups) - 1 else terms[0]
        part = list(contract(plan, groups[n], mine, right[n]))
        return [part[0], swap(part[1])] if plan.split else part

    if not plan.by_pairs:
        return place(plan, groups, order, finish(0))[None]
    parts = [finish(n) for n in range(len(groups) - 1)]
    result = place(plan, groups[:-1], order, [part[v] for v in range(plan.vectors) for part in parts])
    result, right[-1] = lax.optimization_barrier((result, right[-1]))
    return place_last(plan, last, order, finish(len(groups) - 1), result)[None]


def solution(mesh):
    in_specs = (
        P("blk", ("parts", "rows"), None, None),
        P(("parts", "rows"), "blk", None, None),
        P(("parts", "rows"), "blk", None, None),
        P("parts"),
        P(("parts", "rows"), None),
    )
    out_specs = P("blk", ("parts", "rows"), None, None)
    return jax.shard_map(body, mesh=mesh, in_specs=in_specs, out_specs=out_specs, check_vma=False)
```

```python
import functools

import jax
import jax.numpy as jnp
from jax import lax
from jax.experimental import pallas as pl
from jax.experimental.pallas import tpu as pltpu
from jax.sharding import PartitionSpec as P

WACT = 5
MIB = 1024 * 1024
COST = 1000


def smem():
    return pl.BlockSpec(memory_space=pltpu.SMEM)


def vmem():
    return pl.BlockSpec(memory_space=pltpu.VMEM)


def hbm():
    return pl.BlockSpec(memory_space=pltpu.HBM)


class Plan:
    def __init__(self, wave, left_env, devices, cores):
        self.blocks, self.width = wave.shape[1], wave.shape[3]
        self.sectors, self.half = left_env.shape[0], left_env.shape[1]
        self.fan = self.blocks // self.sectors
        self.devices = devices
        self.cap = self.blocks // devices
        self.split = cores == 2 and self.cap % 2 == 0
        self.capc = self.cap // 2 if self.split else self.cap
        self.vectors = 2 if self.split else 1
        self.by_pairs = devices == 8
        if self.by_pairs:
            self.groups = [(0,), (6,), (7,), (1,), (2,), (4,), (3,), (5,)]
        else:
            self.groups = [tuple(range(devices))]

    def partner(self, p):
        return jnp.bitwise_xor(lax.axis_index("rows"), p) if self.by_pairs else jnp.int32(p)

    def rank0(self, core):
        return core * self.capc if self.split else 0


def lists(plan, right_slot):
    devices, blocks, cap, fan, sectors = plan.devices, plan.blocks, plan.cap, plan.fan, plan.sectors
    me = lax.axis_index("rows")
    slots = right_slot.reshape(devices, blocks)
    target = slots // blocks
    index = jnp.arange(blocks, dtype=jnp.int32)
    earlier = (target[:, None, :] == target[:, :, None]) & (index[None, None, :] < index[None, :, None])
    rank = jnp.sum(earlier.astype(jnp.int32), axis=2)
    ranks = jnp.arange(cap, dtype=jnp.int32)
    device = jnp.arange(devices, dtype=jnp.int32)
    value = (device[:, None] * sectors + index[None, :] // fan) * sectors + (slots % blocks) // fan
    hit = (target[:, None, :] == me) & (rank[:, None, :] == ranks[None, :, None])
    code = jnp.sum(jnp.where(hit, value[:, None, :], 0), axis=2)
    my_target = lax.dynamic_slice_in_dim(target, me, 1, axis=0)
    my_rank = lax.dynamic_slice_in_dim(rank, me, 1, axis=0)
    mine = (my_target[:, None, :] == device[:, None, None]) & (my_rank[:, None, :] == ranks[None, :, None])
    order = jnp.sum(jnp.where(mine, index[None, None, :], 0), axis=2)
    return order.astype(jnp.int32).reshape(-1), code.astype(jnp.int32).reshape(-1)


def decode(mask_ref, row, comps, found_ref):
    at = jnp.int32(0)
    for k in range(comps):
        found_ref[at] = jnp.int32(k)
        at = at + mask_ref[row, k]
    return [found_ref[j] for j in range(WACT)]


def each(count, step):
    if count <= 8:
        for s in range(count):
            step(s)
    else:
        pl.loop(0, count)(step)


def slot(plan, group, s):
    if len(group) == 1:
        return group[0], s
    return lax.div(s, plan.capc), lax.rem(s, plan.capc)


def send_kernel(plan, groups, where, masks, code_ref, *rest):
    mask_refs, (own_ref, other_ref) = rest[:masks], rest[masks : masks + 2]
    outs, (found, sem) = rest[masks + 2 : -2], rest[-2:]
    core = lax.axis_index("blk")
    for n, (group, (held, first), out) in enumerate(zip(groups, where, outs)):
        mask_ref = mask_refs[held]

        def step(s):
            p, q = slot(plan, group, s)
            code = code_ref[plan.partner(p) * plan.cap + plan.rank0(core) + q]
            sector = lax.rem(code, plan.sectors)
            row = lax.div(code, plan.sectors)
            if len(group) == 1:
                row = first * plan.sectors + lax.rem(row, plan.sectors)
            for j, k in enumerate(decode(mask_ref, row, 2 * plan.half, found)):
                mine = lax.div(k, plan.half) == core
                at = lax.rem(k, plan.half)

                @pl.when(mine)
                def _():
                    pltpu.make_async_copy(own_ref.at[sector, at], out.at[s, j], sem.at[n]).start()

                @pl.when(jnp.logical_not(mine))
                def _():
                    pltpu.make_async_copy(other_ref.at[sector, at], out.at[s, j], sem.at[n]).start()

        each(len(group) * plan.capc, step)
    for n, out in enumerate(outs):
        pltpu.make_async_copy(out, out, sem.at[n]).wait()


def send(plan, groups, where, code, masks, own, other):
    w, left_comps = plan.width, 2 * plan.half
    return pl.pallas_call(
        functools.partial(send_kernel, plan, groups, where, len(masks)),
        out_shape=[jax.ShapeDtypeStruct((len(g) * plan.capc, WACT, w, w), own.dtype) for g in groups],
        in_specs=[smem()] + [smem() for _ in masks] + [hbm(), hbm()],
        out_specs=[vmem() for _ in groups],
        scratch_shapes=[pltpu.SMEM((left_comps + 1,), jnp.int32), pltpu.SemaphoreType.DMA((len(groups),))],
        compiler_params=pltpu.CompilerParams(vmem_limit_bytes=58 * MIB),
        cost_estimate=pl.CostEstimate(flops=0, bytes_accessed=8_000_000, transcendentals=0),
    )(code, *masks, own, other)


def product_kernel(plan, late, order_ref, mask_ref, own_l, other_l, *rest):
    waves, outs, (left, psi, sem, found) = rest[: plan.vectors], rest[plan.vectors : -4], rest[-4:]
    core = lax.axis_index("blk")
    s = pl.program_id(0)
    w = plan.width

    @pl.when(s == 0)
    def _():
        copies = [
            pltpu.make_async_copy(own_l, left.at[:, pl.ds(core * plan.half, plan.half)], sem.at[0]),
            pltpu.make_async_copy(other_l, left.at[:, pl.ds((1 - core) * plan.half, plan.half)], sem.at[1]),
        ]
        for v in range(plan.vectors):
            copies.append(pltpu.make_async_copy(waves[v], psi.at[v], sem.at[2 + v]))
        for c in copies:
            c.start()
        for c in copies:
            c.wait()

    p, q = lax.div(s, plan.capc), lax.rem(s, plan.capc)
    b = order_ref[plan.partner(p) * plan.cap + plan.rank0(core) + q]
    sector = lax.div(b, plan.fan)
    lhs = jnp.concatenate([left[sector, k] for k in decode(mask_ref, sector, 2 * plan.half, found)], axis=0)
    rhs = jnp.concatenate([psi[v, b] for v in range(plan.vectors)], axis=1)
    terms = jnp.dot(lhs, rhs, preferred_element_type=jnp.float32).astype(jnp.bfloat16)

    def store(out_ref, at):
        for j in range(WACT):
            for v in range(plan.vectors):
                out_ref[at, pl.ds(v * w, w), pl.ds(j * w, w)] = terms[j * w : (j + 1) * w, v * w : (v + 1) * w]

    store(outs[0], 0)
    if late is not None:
        pl.when(p == late)(lambda: store(outs[1], q))


def products(plan, late, order, term_mask, own_l, other_l, waves):
    w, slots = plan.width, plan.devices * plan.capc
    tall, wide = plan.vectors * w, WACT * w
    shapes = [jax.ShapeDtypeStruct((slots, tall, wide), jnp.bfloat16)]
    specs = [pl.BlockSpec((1, tall, wide), lambda s: (s, 0, 0))]
    if late is not None:
        shapes.append(jax.ShapeDtypeStruct((plan.capc, tall, wide), jnp.bfloat16))
        specs.append(pl.BlockSpec((plan.capc, tall, wide), lambda s: (0, 0, 0)))
    return pl.pallas_call(
        functools.partial(product_kernel, plan, late),
        grid=(slots,),
        out_shape=shapes,
        in_specs=[smem(), smem(), hbm(), hbm()] + [hbm() for _ in waves],
        out_specs=specs,
        scratch_shapes=[
            pltpu.VMEM((plan.sectors, 2 * plan.half, w, w), jnp.bfloat16),
            pltpu.VMEM((plan.vectors, plan.blocks, w, w), jnp.bfloat16),
            pltpu.SemaphoreType.DMA((2 + plan.vectors,)),
            pltpu.SMEM((2 * plan.half + 1,), jnp.int32),
        ],
        compiler_params=pltpu.CompilerParams(vmem_limit_bytes=20 * MIB),
        cost_estimate=pl.CostEstimate(flops=COST, bytes_accessed=COST, transcendentals=0),
    )(order, term_mask, own_l, other_l, *waves)


def contract_kernel(plan, terms_ref, right_ref, *outs):
    w = plan.width

    def step(s):
        right = jnp.concatenate([right_ref[s, j] for j in range(WACT)], axis=1)
        done = lax.dot_general(
            terms_ref[s], right, (((1,), (1,)), ((), ())), preferred_element_type=jnp.float32
        ).astype(jnp.bfloat16)
        for v in range(plan.vectors):
            outs[v][s] = done[v * w : (v + 1) * w]

    each(terms_ref.shape[0], step)


def contract(plan, group, terms, right):
    w, count = plan.width, len(group) * plan.capc
    block = min(count, 4)
    first = 0 if terms.shape[0] == count else group[0] * plan.capc // block
    return pl.pallas_call(
        functools.partial(contract_kernel, plan),
        grid=(count // block,),
        out_shape=[jax.ShapeDtypeStruct((count, w, w), jnp.bfloat16) for _ in range(plan.vectors)],
        in_specs=[
            pl.BlockSpec((block, plan.vectors * w, WACT * w), lambda s: (first + s, 0, 0)),
            pl.BlockSpec((block, WACT, w, w), lambda s: (s, 0, 0, 0)),
        ],
        out_specs=[pl.BlockSpec((block, w, w), lambda s: (s, 0, 0)) for _ in range(plan.vectors)],
        compiler_params=pltpu.CompilerParams(vmem_limit_bytes=8 * MIB),
        cost_estimate=pl.CostEstimate(flops=COST, bytes_accessed=COST, transcendentals=0),
    )(terms, right)


def place_kernel(plan, groups, order_ref, *rest):
    n = len(groups)
    parts, out_ref = rest[:-1], rest[-1]
    core = lax.axis_index("blk")
    for v in range(plan.vectors):
        whose = core if v == 0 else 1 - core
        for g, group in enumerate(groups):
            part = parts[v * n + g]

            def step(s):
                p, q = slot(plan, group, s)
                b = order_ref[plan.partner(p) * plan.cap + plan.rank0(whose) + q]
                out_ref[b] = part[s]

            each(len(group) * plan.capc, step)


def place(plan, groups, order, parts):
    w = plan.width
    return pl.pallas_call(
        functools.partial(place_kernel, plan, groups),
        out_shape=jax.ShapeDtypeStruct((plan.blocks, w, w), jnp.bfloat16),
        in_specs=[smem()] + [vmem() for _ in parts],
        out_specs=vmem(),
        compiler_params=pltpu.CompilerParams(vmem_limit_bytes=16 * MIB),
        cost_estimate=pl.CostEstimate(flops=COST, bytes_accessed=COST, transcendentals=0),
    )(order, *parts)


def place_last_kernel(plan, group, order_ref, *rest):
    parts, out_ref, sem = rest[: plan.vectors], rest[-2], rest[-1]
    core = lax.axis_index("blk")
    for wait in (False, True):
        for v in range(plan.vectors):
            whose = core if v == 0 else 1 - core
            for s in range(plan.capc):
                b = order_ref[plan.partner(group[0]) * plan.cap + plan.rank0(whose) + s]
                copy = pltpu.make_async_copy(parts[v].at[s], out_ref.at[b], sem.at[v * plan.capc + s])
                if wait:
                    copy.wait()
                else:
                    copy.start()


def place_last(plan, group, order, parts, result):
    return pl.pallas_call(
        functools.partial(place_last_kernel, plan, group),
        out_shape=jax.ShapeDtypeStruct(result.shape, result.dtype),
        in_specs=[smem()] + [vmem() for _ in parts] + [hbm()],
        out_specs=hbm(),
        scratch_shapes=[pltpu.SemaphoreType.DMA((plan.vectors * plan.capc,))],
        input_output_aliases={1 + plan.vectors: 0},
        compiler_params=pltpu.CompilerParams(vmem_limit_bytes=4 * MIB),
        cost_estimate=pl.CostEstimate(flops=0, bytes_accessed=1_000_000, transcendentals=0),
    )(order, *parts, result)


def body(wave, left_env, right_env, right_slot, term_mask):
    devices = lax.axis_size("rows")
    plan = Plan(wave, left_env, devices, lax.axis_size("blk"))
    swap = functools.partial(lax.ppermute, axis_name="blk", perm=[(0, 1), (1, 0)])

    other_r = swap(right_env)
    order, code = lists(plan, right_slot)
    groups = plan.groups

    def meet(x, group):
        if group == (0,):
            return x
        return lax.ppermute(x, "rows", [(i, i ^ group[0]) for i in range(devices)])

    everyone = functools.partial(lax.all_to_all, axis_name="rows", split_axis=0, concat_axis=0, tiled=True)
    rows, comps = term_mask.shape
    if plan.by_pairs:
        far = [meet(term_mask, (6,)), meet(term_mask, (7,))]
        quad = jnp.concatenate([term_mask, meet(term_mask, (1,)), *far])
        near = meet(quad, (2,))
        urgent = [(6,), (7,)]
        made = dict(zip(urgent, send(plan, urgent, [(0, 0), (1, 0)], code, far, right_env, other_r)))
        code, left_env, wave, made[(6,)] = lax.optimization_barrier((code, left_env, wave, made[(6,)]))
        others = [(1,), (2,), (4,), (3,), (5,), (0,)]
        where = [(0, 1), (1, 0), (1, 2), (1, 1), (1, 3), (0, 0)]
        made.update(zip(others, send(plan, others, where, code, [quad, near], right_env, other_r)))
        after = {(5,): (6,), (1,): (7,)}
        arrived = {}
        for g in groups:
            x = made[g]
            if g in after:
                x, arrived[after[g]] = lax.optimization_barrier((x, arrived[after[g]]))
            arrived[g] = meet(x, g)
        right = [arrived[g] for g in groups]
    else:
        wide = jnp.broadcast_to(term_mask[None], (devices, rows, comps)).reshape(-1, comps)
        sent = send(plan, groups, [(0, 0)], code, [everyone(wide)], right_env, other_r)
        right = [everyone(sent[0])]

    other_l = swap(left_env)
    waves = [wave[0]] + ([swap(wave[0])] if plan.split else [])
    last = groups[-1]
    terms = products(plan, last[0] if plan.by_pairs else None, order, term_mask, left_env, other_l, waves)

    def finish(n):
        mine = terms[1] if plan.by_pairs and n == len(groups) - 1 else terms[0]
        part = list(contract(plan, groups[n], mine, right[n]))
        return [part[0], swap(part[1])] if plan.split else part

    if not plan.by_pairs:
        return place(plan, groups, order, finish(0))[None]
    parts = [finish(n) for n in range(len(groups) - 1)]
    result = place(plan, groups[:-1], order, [part[v] for v in range(plan.vectors) for part in parts])
    result, right[-1] = lax.optimization_barrier((result, right[-1]))
    return place_last(plan, last, order, finish(len(groups) - 1), result)[None]


def solution(mesh):
    in_specs = (
        P("blk", ("parts", "rows"), None, None),
        P(("parts", "rows"), "blk", None, None),
        P(("parts", "rows"), "blk", None, None),
        P("parts"),
        P(("parts", "rows"), None),
    )
    out_specs = P("blk", ("parts", "rows"), None, None)
    return jax.shard_map(body, mesh=mesh, in_specs=in_specs, out_specs=out_specs, check_vma=False)
```

```python
import functools

import jax
import jax.numpy as jnp
from jax import lax
from jax.experimental import pallas as pl
from jax.experimental.pallas import tpu as pltpu
from jax.sharding import PartitionSpec as P

WACT = 5
MIB = 1024 * 1024
COST = 1000


def smem():
    return pl.BlockSpec(memory_space=pltpu.SMEM)


def vmem():
    return pl.BlockSpec(memory_space=pltpu.VMEM)


def hbm():
    return pl.BlockSpec(memory_space=pltpu.HBM)


class Plan:
    def __init__(self, wave, left_env, devices, cores):
        self.blocks, self.width = wave.shape[1], wave.shape[3]
        self.sectors, self.half = left_env.shape[0], left_env.shape[1]
        self.fan = self.blocks // self.sectors
        self.devices = devices
        self.cap = self.blocks // devices
        self.split = cores == 2 and self.cap % 2 == 0
        self.capc = self.cap // 2 if self.split else self.cap
        self.vectors = 2 if self.split else 1
        self.by_pairs = devices == 8
        if self.by_pairs:
            self.groups = [(0,), (6,), (7,), (1,), (2,), (4,), (3,), (5,)]
        else:
            self.groups = [tuple(range(devices))]

    def partner(self, p):
        return jnp.bitwise_xor(lax.axis_index("rows"), p) if self.by_pairs else jnp.int32(p)

    def rank0(self, core):
        return core * self.capc if self.split else 0


def lists(plan, right_slot):
    devices, blocks, cap, fan, sectors = plan.devices, plan.blocks, plan.cap, plan.fan, plan.sectors
    me = lax.axis_index("rows")
    slots = right_slot.reshape(devices, blocks)
    target = slots // blocks
    index = jnp.arange(blocks, dtype=jnp.int32)
    earlier = (target[:, None, :] == target[:, :, None]) & (index[None, None, :] < index[None, :, None])
    rank = jnp.sum(earlier.astype(jnp.int32), axis=2)
    ranks = jnp.arange(cap, dtype=jnp.int32)
    device = jnp.arange(devices, dtype=jnp.int32)
    value = (device[:, None] * sectors + index[None, :] // fan) * sectors + (slots % blocks) // fan
    hit = (target[:, None, :] == me) & (rank[:, None, :] == ranks[None, :, None])
    code = jnp.sum(jnp.where(hit, value[:, None, :], 0), axis=2)
    my_target = lax.dynamic_slice_in_dim(target, me, 1, axis=0)
    my_rank = lax.dynamic_slice_in_dim(rank, me, 1, axis=0)
    mine = (my_target[:, None, :] == device[:, None, None]) & (my_rank[:, None, :] == ranks[None, :, None])
    order = jnp.sum(jnp.where(mine, index[None, None, :], 0), axis=2)
    return order.astype(jnp.int32).reshape(-1), code.astype(jnp.int32).reshape(-1)


def decode(mask_ref, row, comps, found_ref):
    at = jnp.int32(0)
    for k in range(comps):
        found_ref[at] = jnp.int32(k)
        at = at + mask_ref[row, k]
    return [found_ref[j] for j in range(WACT)]


def each(count, step):
    if count <= 8:
        for s in range(count):
            step(s)
    else:
        pl.loop(0, count)(step)


def slot(plan, group, s):
    if len(group) == 1:
        return group[0], s
    return lax.div(s, plan.capc), lax.rem(s, plan.capc)


def send_kernel(plan, groups, where, masks, code_ref, *rest):
    mask_refs, (own_ref, other_ref) = rest[:masks], rest[masks : masks + 2]
    n = len(groups)
    outs, held, (found, sem) = rest[masks + 2 : masks + 2 + n], rest[masks + 2 + n : -2], rest[-2:]
    core = lax.axis_index("blk")
    for n, (group, (which, first), out) in enumerate(zip(groups, where, held)):
        mask_ref = mask_refs[which]

        def step(s):
            p, q = slot(plan, group, s)
            code = code_ref[plan.partner(p) * plan.cap + plan.rank0(core) + q]
            sector = lax.rem(code, plan.sectors)
            row = lax.div(code, plan.sectors)
            if len(group) == 1:
                row = first * plan.sectors + lax.rem(row, plan.sectors)
            for j, k in enumerate(decode(mask_ref, row, 2 * plan.half, found)):
                mine = lax.div(k, plan.half) == core
                at = lax.rem(k, plan.half)

                @pl.when(mine)
                def _():
                    pltpu.make_async_copy(own_ref.at[sector, at], out.at[s, j], sem.at[n]).start()

                @pl.when(jnp.logical_not(mine))
                def _():
                    pltpu.make_async_copy(other_ref.at[sector, at], out.at[s, j], sem.at[n]).start()

        each(len(group) * plan.capc, step)
    copies = []
    for n, (out, mine) in enumerate(zip(outs, held)):
        pltpu.make_async_copy(mine, mine, sem.at[n]).wait()
        copies.append(pltpu.make_async_copy(mine, out, sem.at[len(groups) + n]))
        copies[-1].start()
    for copy in copies:
        copy.wait()


def send(plan, groups, where, code, masks, own, other):
    w, left_comps = plan.width, 2 * plan.half
    return pl.pallas_call(
        functools.partial(send_kernel, plan, groups, where, len(masks)),
        out_shape=[jax.ShapeDtypeStruct((len(g) * plan.capc, WACT, w, w), own.dtype) for g in groups],
        in_specs=[smem()] + [smem() for _ in masks] + [hbm(), hbm()],
        out_specs=[hbm() for _ in groups],
        scratch_shapes=[pltpu.VMEM((len(g) * plan.capc, WACT, w, w), own.dtype) for g in groups]
        + [pltpu.SMEM((left_comps + 1,), jnp.int32), pltpu.SemaphoreType.DMA((2 * len(groups),))],
        compiler_params=pltpu.CompilerParams(vmem_limit_bytes=(52 if len(groups) == 2 else 58) * MIB),
        cost_estimate=pl.CostEstimate(flops=0, bytes_accessed=8_000_000, transcendentals=0),
    )(code, *masks, own, other)


def product_kernel(plan, late, order_ref, mask_ref, own_l, other_l, *rest):
    waves, outs, (left, psi, sem, found) = rest[: plan.vectors], rest[plan.vectors : -4], rest[-4:]
    core = lax.axis_index("blk")
    s = pl.program_id(0)
    w = plan.width

    @pl.when(s == 0)
    def _():
        copies = [
            pltpu.make_async_copy(own_l, left.at[:, pl.ds(core * plan.half, plan.half)], sem.at[0]),
            pltpu.make_async_copy(other_l, left.at[:, pl.ds((1 - core) * plan.half, plan.half)], sem.at[1]),
        ]
        for v in range(plan.vectors):
            copies.append(pltpu.make_async_copy(waves[v], psi.at[v], sem.at[2 + v]))
        for c in copies:
            c.start()
        for c in copies:
            c.wait()

    p, q = lax.div(s, plan.capc), lax.rem(s, plan.capc)
    b = order_ref[plan.partner(p) * plan.cap + plan.rank0(core) + q]
    sector = lax.div(b, plan.fan)
    lhs = jnp.concatenate([left[sector, k] for k in decode(mask_ref, sector, 2 * plan.half, found)], axis=0)
    rhs = jnp.concatenate([psi[v, b] for v in range(plan.vectors)], axis=1)
    terms = jnp.dot(lhs, rhs, preferred_element_type=jnp.float32).astype(jnp.bfloat16)

    def store(out_ref, at):
        for j in range(WACT):
            for v in range(plan.vectors):
                out_ref[at, pl.ds(v * w, w), pl.ds(j * w, w)] = terms[j * w : (j + 1) * w, v * w : (v + 1) * w]

    store(outs[0], 0)
    if late is not None:
        pl.when(p == late)(lambda: store(outs[1], q))


def products(plan, late, order, term_mask, own_l, other_l, waves):
    w, slots = plan.width, plan.devices * plan.capc
    tall, wide = plan.vectors * w, WACT * w
    shapes = [jax.ShapeDtypeStruct((slots, tall, wide), jnp.bfloat16)]
    specs = [pl.BlockSpec((1, tall, wide), lambda s: (s, 0, 0))]
    if late is not None:
        shapes.append(jax.ShapeDtypeStruct((plan.capc, tall, wide), jnp.bfloat16))
        specs.append(pl.BlockSpec((plan.capc, tall, wide), lambda s: (0, 0, 0)))
    return pl.pallas_call(
        functools.partial(product_kernel, plan, late),
        grid=(slots,),
        out_shape=shapes,
        in_specs=[smem(), smem(), hbm(), hbm()] + [hbm() for _ in waves],
        out_specs=specs,
        scratch_shapes=[
            pltpu.VMEM((plan.sectors, 2 * plan.half, w, w), jnp.bfloat16),
            pltpu.VMEM((plan.vectors, plan.blocks, w, w), jnp.bfloat16),
            pltpu.SemaphoreType.DMA((2 + plan.vectors,)),
            pltpu.SMEM((2 * plan.half + 1,), jnp.int32),
        ],
        compiler_params=pltpu.CompilerParams(vmem_limit_bytes=20 * MIB),
        cost_estimate=pl.CostEstimate(flops=COST, bytes_accessed=COST, transcendentals=0),
    )(order, term_mask, own_l, other_l, *waves)


def contract_kernel(plan, terms_ref, right_ref, *outs):
    w = plan.width

    def step(s):
        right = jnp.concatenate([right_ref[s, j] for j in range(WACT)], axis=1)
        done = lax.dot_general(
            terms_ref[s], right, (((1,), (1,)), ((), ())), preferred_element_type=jnp.float32
        ).astype(jnp.bfloat16)
        for v in range(plan.vectors):
            outs[v][s] = done[v * w : (v + 1) * w]

    each(terms_ref.shape[0], step)


def contract(plan, group, terms, right):
    w, count = plan.width, len(group) * plan.capc
    block = min(count, 4)
    first = 0 if terms.shape[0] == count else group[0] * plan.capc // block
    return pl.pallas_call(
        functools.partial(contract_kernel, plan),
        grid=(count // block,),
        out_shape=[jax.ShapeDtypeStruct((count, w, w), jnp.bfloat16) for _ in range(plan.vectors)],
        in_specs=[
            pl.BlockSpec((block, plan.vectors * w, WACT * w), lambda s: (first + s, 0, 0)),
            pl.BlockSpec((block, WACT, w, w), lambda s: (s, 0, 0, 0)),
        ],
        out_specs=[pl.BlockSpec((block, w, w), lambda s: (s, 0, 0)) for _ in range(plan.vectors)],
        compiler_params=pltpu.CompilerParams(vmem_limit_bytes=8 * MIB),
        cost_estimate=pl.CostEstimate(flops=COST, bytes_accessed=COST, transcendentals=0),
    )(terms, right)


def place_kernel(plan, groups, order_ref, *rest):
    n = len(groups)
    parts, out_ref = rest[:-1], rest[-1]
    core = lax.axis_index("blk")
    for v in range(plan.vectors):
        whose = core if v == 0 else 1 - core
        for g, group in enumerate(groups):
            part = parts[v * n + g]

            def step(s):
                p, q = slot(plan, group, s)
                b = order_ref[plan.partner(p) * plan.cap + plan.rank0(whose) + q]
                out_ref[b] = part[s]

            each(len(group) * plan.capc, step)


def place(plan, groups, order, parts):
    w = plan.width
    return pl.pallas_call(
        functools.partial(place_kernel, plan, groups),
        out_shape=jax.ShapeDtypeStruct((plan.blocks, w, w), jnp.bfloat16),
        in_specs=[smem()] + [vmem() for _ in parts],
        out_specs=vmem(),
        compiler_params=pltpu.CompilerParams(vmem_limit_bytes=16 * MIB),
        cost_estimate=pl.CostEstimate(flops=COST, bytes_accessed=COST, transcendentals=0),
    )(order, *parts)


def place_last_kernel(plan, group, order_ref, *rest):
    parts, out_ref, sem = rest[: plan.vectors], rest[-2], rest[-1]
    core = lax.axis_index("blk")
    for wait in (False, True):
        for v in range(plan.vectors):
            whose = core if v == 0 else 1 - core
            for s in range(plan.capc):
                b = order_ref[plan.partner(group[0]) * plan.cap + plan.rank0(whose) + s]
                copy = pltpu.make_async_copy(parts[v].at[s], out_ref.at[b], sem.at[v * plan.capc + s])
                if wait:
                    copy.wait()
                else:
                    copy.start()


def place_last(plan, group, order, parts, result):
    return pl.pallas_call(
        functools.partial(place_last_kernel, plan, group),
        out_shape=jax.ShapeDtypeStruct(result.shape, result.dtype),
        in_specs=[smem()] + [vmem() for _ in parts] + [hbm()],
        out_specs=hbm(),
        scratch_shapes=[pltpu.SemaphoreType.DMA((plan.vectors * plan.capc,))],
        input_output_aliases={1 + plan.vectors: 0},
        compiler_params=pltpu.CompilerParams(vmem_limit_bytes=4 * MIB),
        cost_estimate=pl.CostEstimate(flops=0, bytes_accessed=1_000_000, transcendentals=0),
    )(order, *parts, result)


def body(wave, left_env, right_env, right_slot, term_mask):
    devices = lax.axis_size("rows")
    plan = Plan(wave, left_env, devices, lax.axis_size("blk"))
    swap = functools.partial(lax.ppermute, axis_name="blk", perm=[(0, 1), (1, 0)])

    other_r = swap(right_env)
    order, code = lists(plan, right_slot)
    groups = plan.groups

    def meet(x, group):
        if group == (0,):
            return x
        return lax.ppermute(x, "rows", [(i, i ^ group[0]) for i in range(devices)])

    everyone = functools.partial(lax.all_to_all, axis_name="rows", split_axis=0, concat_axis=0, tiled=True)
    rows, comps = term_mask.shape
    if plan.by_pairs:
        far = [meet(term_mask, (6,)), meet(term_mask, (7,))]
        quad = jnp.concatenate([term_mask, meet(term_mask, (1,)), *far])
        near = meet(quad, (2,))
        urgent = [(6,), (7,)]
        made = dict(zip(urgent, send(plan, urgent, [(0, 0), (1, 0)], code, far, right_env, other_r)))
        code, left_env, wave, made[(6,)] = lax.optimization_barrier((code, left_env, wave, made[(6,)]))
        others = [(1,), (2,), (4,), (3,), (5,), (0,)]
        where = [(0, 1), (1, 0), (1, 2), (1, 1), (1, 3), (0, 0)]
        made.update(zip(others, send(plan, others, where, code, [quad, near], right_env, other_r)))
        after = {(5,): (6,), (1,): (7,)}
        arrived = {}
        for g in groups:
            x = made[g]
            if g in after:
                x, arrived[after[g]] = lax.optimization_barrier((x, arrived[after[g]]))
            arrived[g] = meet(x, g)
        right = [arrived[g] for g in groups]
    else:
        wide = jnp.broadcast_to(term_mask[None], (devices, rows, comps)).reshape(-1, comps)
        sent = send(plan, groups, [(0, 0)], code, [everyone(wide)], right_env, other_r)
        right = [everyone(sent[0])]

    other_l = swap(left_env)
    waves = [wave[0]] + ([swap(wave[0])] if plan.split else [])
    last = groups[-1]
    terms = products(plan, last[0] if plan.by_pairs else None, order, term_mask, left_env, other_l, waves)

    def finish(n):
        mine = terms[1] if plan.by_pairs and n == len(groups) - 1 else terms[0]
        part = list(contract(plan, groups[n], mine, right[n]))
        return [part[0], swap(part[1])] if plan.split else part

    if not plan.by_pairs:
        return place(plan, groups, order, finish(0))[None]
    parts = [finish(n) for n in range(len(groups) - 1)]
    result = place(plan, groups[:-1], order, [part[v] for v in range(plan.vectors) for part in parts])
    result, right[-1] = lax.optimization_barrier((result, right[-1]))
    return place_last(plan, last, order, finish(len(groups) - 1), result)[None]


def solution(mesh):
    in_specs = (
        P("blk", ("parts", "rows"), None, None),
        P(("parts", "rows"), "blk", None, None),
        P(("parts", "rows"), "blk", None, None),
        P("parts"),
        P(("parts", "rows"), None),
    )
    out_specs = P("blk", ("parts", "rows"), None, None)
    return jax.shard_map(body, mesh=mesh, in_specs=in_specs, out_specs=out_specs, check_vma=False)
```

```python
import functools

import jax
import jax.numpy as jnp
from jax import lax
from jax.experimental import pallas as pl
from jax.experimental.pallas import tpu as pltpu
from jax.sharding import PartitionSpec as P

WACT = 5
MIB = 1024 * 1024
COST = 1000


def smem():
    return pl.BlockSpec(memory_space=pltpu.SMEM)


def vmem():
    return pl.BlockSpec(memory_space=pltpu.VMEM)


def hbm():
    return pl.BlockSpec(memory_space=pltpu.HBM)


class Plan:
    def __init__(self, wave, left_env, devices, cores):
        self.blocks, self.width = wave.shape[1], wave.shape[3]
        self.sectors, self.half = left_env.shape[0], left_env.shape[1]
        self.fan = self.blocks // self.sectors
        self.devices = devices
        self.cap = self.blocks // devices
        self.split = cores == 2 and self.cap % 2 == 0
        self.capc = self.cap // 2 if self.split else self.cap
        self.vectors = 2 if self.split else 1
        self.by_pairs = devices == 8
        if self.by_pairs:
            self.groups = [(0,), (6,), (7,), (1,), (2,), (4,), (3,), (5,)]
        else:
            self.groups = [tuple(range(devices))]

    def partner(self, p):
        return jnp.bitwise_xor(lax.axis_index("rows"), p) if self.by_pairs else jnp.int32(p)

    def rank0(self, core):
        return core * self.capc if self.split else 0


def lists(plan, right_slot):
    devices, blocks, cap, fan, sectors = plan.devices, plan.blocks, plan.cap, plan.fan, plan.sectors
    me = lax.axis_index("rows")
    slots = right_slot.reshape(devices, blocks)
    target = slots // blocks
    index = jnp.arange(blocks, dtype=jnp.int32)
    earlier = (target[:, None, :] == target[:, :, None]) & (index[None, None, :] < index[None, :, None])
    rank = jnp.sum(earlier.astype(jnp.int32), axis=2)
    ranks = jnp.arange(cap, dtype=jnp.int32)
    device = jnp.arange(devices, dtype=jnp.int32)
    value = (device[:, None] * sectors + index[None, :] // fan) * sectors + (slots % blocks) // fan
    hit = (target[:, None, :] == me) & (rank[:, None, :] == ranks[None, :, None])
    code = jnp.sum(jnp.where(hit, value[:, None, :], 0), axis=2)
    my_target = lax.dynamic_slice_in_dim(target, me, 1, axis=0)
    my_rank = lax.dynamic_slice_in_dim(rank, me, 1, axis=0)
    mine = (my_target[:, None, :] == device[:, None, None]) & (my_rank[:, None, :] == ranks[None, :, None])
    order = jnp.sum(jnp.where(mine, index[None, None, :], 0), axis=2)
    return order.astype(jnp.int32).reshape(-1), code.astype(jnp.int32).reshape(-1)


def decode(mask_ref, row, comps, found_ref):
    at = jnp.int32(0)
    for k in range(comps):
        found_ref[at] = jnp.int32(k)
        at = at + mask_ref[row, k]
    return [found_ref[j] for j in range(WACT)]


def each(count, step):
    if count <= 8:
        for s in range(count):
            step(s)
    else:
        pl.loop(0, count)(step)


def slot(plan, group, s):
    if len(group) == 1:
        return group[0], s
    return lax.div(s, plan.capc), lax.rem(s, plan.capc)


def send_kernel(plan, groups, where, masks, code_ref, *rest):
    mask_refs, (own_ref, other_ref) = rest[:masks], rest[masks : masks + 2]
    n = len(groups)
    outs, held, (found, sem) = rest[masks + 2 : masks + 2 + n], rest[masks + 2 + n : -2], rest[-2:]
    core = lax.axis_index("blk")
    for n, (group, (which, first), out) in enumerate(zip(groups, where, held)):
        mask_ref = mask_refs[which]

        def step(s):
            p, q = slot(plan, group, s)
            code = code_ref[plan.partner(p) * plan.cap + plan.rank0(core) + q]
            sector = lax.rem(code, plan.sectors)
            row = lax.div(code, plan.sectors)
            if len(group) == 1:
                row = first * plan.sectors + lax.rem(row, plan.sectors)
            for j, k in enumerate(decode(mask_ref, row, 2 * plan.half, found)):
                mine = lax.div(k, plan.half) == core
                at = lax.rem(k, plan.half)

                @pl.when(mine)
                def _():
                    pltpu.make_async_copy(own_ref.at[sector, at], out.at[s, j], sem.at[n]).start()

                @pl.when(jnp.logical_not(mine))
                def _():
                    pltpu.make_async_copy(other_ref.at[sector, at], out.at[s, j], sem.at[n]).start()

        each(len(group) * plan.capc, step)
    copies = []
    for n, (out, mine) in enumerate(zip(outs, held)):
        pltpu.make_async_copy(mine, mine, sem.at[n]).wait()
        copies.append(pltpu.make_async_copy(mine, out, sem.at[len(groups) + n]))
        copies[-1].start()
    for copy in copies:
        copy.wait()


def send(plan, groups, where, code, masks, own, other):
    w, left_comps = plan.width, 2 * plan.half
    return pl.pallas_call(
        functools.partial(send_kernel, plan, groups, where, len(masks)),
        out_shape=[jax.ShapeDtypeStruct((len(g) * plan.capc, WACT, w, w), own.dtype) for g in groups],
        in_specs=[smem()] + [smem() for _ in masks] + [hbm(), hbm()],
        out_specs=[hbm() for _ in groups],
        scratch_shapes=[pltpu.VMEM((len(g) * plan.capc, WACT, w, w), own.dtype) for g in groups]
        + [pltpu.SMEM((left_comps + 1,), jnp.int32), pltpu.SemaphoreType.DMA((2 * len(groups),))],
        compiler_params=pltpu.CompilerParams(vmem_limit_bytes=(52 if len(groups) == 2 else 58) * MIB),
        cost_estimate=pl.CostEstimate(flops=0, bytes_accessed=8_000_000, transcendentals=0),
    )(code, *masks, own, other)


def product_kernel(plan, late, order_ref, mask_ref, own_l, other_l, *rest):
    waves, outs, (left, psi, sem, found) = rest[: plan.vectors], rest[plan.vectors : -4], rest[-4:]
    core = lax.axis_index("blk")
    s = pl.program_id(0)
    w = plan.width

    @pl.when(s == 0)
    def _():
        copies = [
            pltpu.make_async_copy(own_l, left.at[:, pl.ds(core * plan.half, plan.half)], sem.at[0]),
            pltpu.make_async_copy(other_l, left.at[:, pl.ds((1 - core) * plan.half, plan.half)], sem.at[1]),
        ]
        for v in range(plan.vectors):
            copies.append(pltpu.make_async_copy(waves[v], psi.at[v], sem.at[2 + v]))
        for c in copies:
            c.start()
        for c in copies:
            c.wait()

    p, q = lax.div(s, plan.capc), lax.rem(s, plan.capc)
    b = order_ref[plan.partner(p) * plan.cap + plan.rank0(core) + q]
    sector = lax.div(b, plan.fan)
    lhs = jnp.concatenate([left[sector, k] for k in decode(mask_ref, sector, 2 * plan.half, found)], axis=0)
    rhs = jnp.concatenate([psi[v, b] for v in range(plan.vectors)], axis=1)
    terms = jnp.dot(lhs, rhs, preferred_element_type=jnp.float32).astype(jnp.bfloat16)

    def store(out_ref, at):
        for j in range(WACT):
            for v in range(plan.vectors):
                out_ref[at, pl.ds(v * w, w), pl.ds(j * w, w)] = terms[j * w : (j + 1) * w, v * w : (v + 1) * w]

    store(outs[0], 0)
    if late is not None:
        pl.when(p == late)(lambda: store(outs[1], q))


def products(plan, late, order, term_mask, own_l, other_l, waves):
    w, slots = plan.width, plan.devices * plan.capc
    tall, wide = plan.vectors * w, WACT * w
    shapes = [jax.ShapeDtypeStruct((slots, tall, wide), jnp.bfloat16)]
    specs = [pl.BlockSpec((1, tall, wide), lambda s: (s, 0, 0))]
    if late is not None:
        shapes.append(jax.ShapeDtypeStruct((plan.capc, tall, wide), jnp.bfloat16))
        specs.append(pl.BlockSpec((plan.capc, tall, wide), lambda s: (0, 0, 0)))
    return pl.pallas_call(
        functools.partial(product_kernel, plan, late),
        grid=(slots,),
        out_shape=shapes,
        in_specs=[smem(), smem(), hbm(), hbm()] + [hbm() for _ in waves],
        out_specs=specs,
        scratch_shapes=[
            pltpu.VMEM((plan.sectors, 2 * plan.half, w, w), jnp.bfloat16),
            pltpu.VMEM((plan.vectors, plan.blocks, w, w), jnp.bfloat16),
            pltpu.SemaphoreType.DMA((2 + plan.vectors,)),
            pltpu.SMEM((2 * plan.half + 1,), jnp.int32),
        ],
        compiler_params=pltpu.CompilerParams(vmem_limit_bytes=20 * MIB),
        cost_estimate=pl.CostEstimate(flops=COST, bytes_accessed=COST, transcendentals=0),
    )(order, term_mask, own_l, other_l, *waves)


def contract_kernel(plan, terms_ref, right_ref, *outs):
    w = plan.width

    def step(s):
        right = jnp.concatenate([right_ref[s, j] for j in range(WACT)], axis=1)
        done = lax.dot_general(
            terms_ref[s], right, (((1,), (1,)), ((), ())), preferred_element_type=jnp.float32
        ).astype(jnp.bfloat16)
        for v in range(plan.vectors):
            outs[v][s] = done[v * w : (v + 1) * w]

    each(terms_ref.shape[0], step)


def contract(plan, group, terms, right):
    w, count = plan.width, len(group) * plan.capc
    block = min(count, 4 if terms.shape[0] == count else 2)
    first = 0 if terms.shape[0] == count else group[0] * plan.capc // block
    return pl.pallas_call(
        functools.partial(contract_kernel, plan),
        grid=(count // block,),
        out_shape=[jax.ShapeDtypeStruct((count, w, w), jnp.bfloat16) for _ in range(plan.vectors)],
        in_specs=[
            pl.BlockSpec((block, plan.vectors * w, WACT * w), lambda s: (first + s, 0, 0)),
            pl.BlockSpec((block, WACT, w, w), lambda s: (s, 0, 0, 0)),
        ],
        out_specs=[pl.BlockSpec((block, w, w), lambda s: (s, 0, 0)) for _ in range(plan.vectors)],
        compiler_params=pltpu.CompilerParams(vmem_limit_bytes=8 * MIB),
        cost_estimate=pl.CostEstimate(flops=COST, bytes_accessed=COST, transcendentals=0),
    )(terms, right)


def place_kernel(plan, groups, order_ref, *rest):
    n = len(groups)
    parts, out_ref = rest[:-1], rest[-1]
    core = lax.axis_index("blk")
    for v in range(plan.vectors):
        whose = core if v == 0 else 1 - core
        for g, group in enumerate(groups):
            part = parts[v * n + g]

            def step(s):
                p, q = slot(plan, group, s)
                b = order_ref[plan.partner(p) * plan.cap + plan.rank0(whose) + q]
                out_ref[b] = part[s]

            each(len(group) * plan.capc, step)


def place(plan, groups, order, parts):
    w = plan.width
    return pl.pallas_call(
        functools.partial(place_kernel, plan, groups),
        out_shape=jax.ShapeDtypeStruct((plan.blocks, w, w), jnp.bfloat16),
        in_specs=[smem()] + [vmem() for _ in parts],
        out_specs=vmem(),
        compiler_params=pltpu.CompilerParams(vmem_limit_bytes=16 * MIB),
        cost_estimate=pl.CostEstimate(flops=COST, bytes_accessed=COST, transcendentals=0),
    )(order, *parts)


def place_last_kernel(plan, group, order_ref, *rest):
    parts, out_ref, sem = rest[: plan.vectors], rest[-2], rest[-1]
    core = lax.axis_index("blk")
    for wait in (False, True):
        for v in range(plan.vectors):
            whose = core if v == 0 else 1 - core
            for s in range(plan.capc):
                b = order_ref[plan.partner(group[0]) * plan.cap + plan.rank0(whose) + s]
                copy = pltpu.make_async_copy(parts[v].at[s], out_ref.at[b], sem.at[v * plan.capc + s])
                if wait:
                    copy.wait()
                else:
                    copy.start()


def place_last(plan, group, order, parts, result):
    return pl.pallas_call(
        functools.partial(place_last_kernel, plan, group),
        out_shape=jax.ShapeDtypeStruct(result.shape, result.dtype),
        in_specs=[smem()] + [vmem() for _ in parts] + [hbm()],
        out_specs=hbm(),
        scratch_shapes=[pltpu.SemaphoreType.DMA((plan.vectors * plan.capc,))],
        input_output_aliases={1 + plan.vectors: 0},
        compiler_params=pltpu.CompilerParams(vmem_limit_bytes=4 * MIB),
        cost_estimate=pl.CostEstimate(flops=0, bytes_accessed=1_000_000, transcendentals=0),
    )(order, *parts, result)


def body(wave, left_env, right_env, right_slot, term_mask):
    devices = lax.axis_size("rows")
    plan = Plan(wave, left_env, devices, lax.axis_size("blk"))
    swap = functools.partial(lax.ppermute, axis_name="blk", perm=[(0, 1), (1, 0)])

    other_r = swap(right_env)
    order, code = lists(plan, right_slot)
    groups = plan.groups

    def meet(x, group):
        if group == (0,):
            return x
        return lax.ppermute(x, "rows", [(i, i ^ group[0]) for i in range(devices)])

    everyone = functools.partial(lax.all_to_all, axis_name="rows", split_axis=0, concat_axis=0, tiled=True)
    rows, comps = term_mask.shape
    if plan.by_pairs:
        far = [meet(term_mask, (6,)), meet(term_mask, (7,))]
        quad = jnp.concatenate([term_mask, meet(term_mask, (1,)), *far])
        near = meet(quad, (2,))
        urgent = [(6,), (7,)]
        made = dict(zip(urgent, send(plan, urgent, [(0, 0), (1, 0)], code, far, right_env, other_r)))
        code, left_env, wave, made[(6,)] = lax.optimization_barrier((code, left_env, wave, made[(6,)]))
        others = [(1,), (2,), (4,), (3,), (5,), (0,)]
        where = [(0, 1), (1, 0), (1, 2), (1, 1), (1, 3), (0, 0)]
        made.update(zip(others, send(plan, others, where, code, [quad, near], right_env, other_r)))
        after = {(5,): (6,), (1,): (7,)}
        arrived = {}
        for g in groups:
            x = made[g]
            if g in after:
                x, arrived[after[g]] = lax.optimization_barrier((x, arrived[after[g]]))
            arrived[g] = meet(x, g)
        right = [arrived[g] for g in groups]
    else:
        wide = jnp.broadcast_to(term_mask[None], (devices, rows, comps)).reshape(-1, comps)
        sent = send(plan, groups, [(0, 0)], code, [everyone(wide)], right_env, other_r)
        right = [everyone(sent[0])]

    other_l = swap(left_env)
    waves = [wave[0]] + ([swap(wave[0])] if plan.split else [])
    last = groups[-1]
    terms = products(plan, last[0] if plan.by_pairs else None, order, term_mask, left_env, other_l, waves)

    def finish(n):
        mine = terms[1] if plan.by_pairs and n == len(groups) - 1 else terms[0]
        part = list(contract(plan, groups[n], mine, right[n]))
        return [part[0], swap(part[1])] if plan.split else part

    if not plan.by_pairs:
        return place(plan, groups, order, finish(0))[None]
    parts = [finish(n) for n in range(len(groups) - 1)]
    result = place(plan, groups[:-1], order, [part[v] for v in range(plan.vectors) for part in parts])
    result, right[-1] = lax.optimization_barrier((result, right[-1]))
    return place_last(plan, last, order, finish(len(groups) - 1), result)[None]


def solution(mesh):
    in_specs = (
        P("blk", ("parts", "rows"), None, None),
        P(("parts", "rows"), "blk", None, None),
        P(("parts", "rows"), "blk", None, None),
        P("parts"),
        P(("parts", "rows"), None),
    )
    out_specs = P("blk", ("parts", "rows"), None, None)
    return jax.shard_map(body, mesh=mesh, in_specs=in_specs, out_specs=out_specs, check_vma=False)
```
